256 devices in a mesh: gossip: 128 (over x_lo, y, z, core), dp: 2 (over x_hi).
Axes of the slice: x: 4 (x_hi: 2, x_lo: 2; x = x_hi * 2 + x_lo), y: 4, z: 8, core: 2. Of those that a mesh axis runs over, the one named last changes fastest.
Arguments:
- images: bfloat16 [256, 28, 28, 512], P(('gossip', 'dp')), may hold values from -6 to 6
- cotangent: bfloat16 [256, 28, 28, 512], P(('gossip', 'dp')), may hold values from -6 to 6
- w_first: float32 [128, 512, 128], P('gossip', 'dp'), may hold values from -6 to 6
- w_middle: float32 [128, 1152, 128], P('gossip', 'dp'), may hold values from -6 to 6
- w_last: float32 [128, 128, 512], P('gossip', None, 'dp'), may hold values from -6 to 6
- m_first: float32 [128, 512, 128], P('gossip', 'dp'), may hold values from -6 to 6
- m_middle: float32 [128, 1152, 128], P('gossip', 'dp'), may hold values from -6 to 6
- m_last: float32 [128, 128, 512], P('gossip', None, 'dp'), may hold values from -6 to 6
Outputs:
- new_first: float32 [128, 512, 128], P('gossip', 'dp')
- new_middle: float32 [128, 1152, 128], P('gossip', 'dp')
- new_last: float32 [128, 128, 512], P('gossip', None, 'dp')
- mom_first: float32 [128, 512, 128], P('gossip', 'dp')
- mom_middle: float32 [128, 1152, 128], P('gossip', 'dp')
- mom_last: float32 [128, 128, 512], P('gossip', None, 'dp')
The draws below stay inside these ranges and needn't reach their ends.
All inputs are finite; a program needn't handle non-finite values.
Results may differ from the reference program's by a relative error of at most 0.0065.
Values may be sent and summed in bfloat16 or wider, within the bound.
A program may use at most 64 MiB of HBM per device.

```python
import jax
import jax.numpy as jnp
from jax import lax

CIN = 512
MID = 128
SIDE = 28
IMG_DEV = 1
REPLICAS = 128
IMAGES = 256
N_GOSSIP = 128
N_DP = 2


def steps_of(own_key, shape, shards, least, largest):
    gain = 1.0
    for axis_at, blocks in shards:
        heights = jax.random.uniform(jax.random.fold_in(jax.random.fold_in(own_key, 6), axis_at), (blocks,), jnp.float32, least / len(shards), largest / len(shards))
        gain = gain * jnp.repeat(jnp.exp(heights), shape[axis_at] // blocks).reshape((-1,) + (1,) * (len(shape) - 1 - axis_at))
    return gain


def noise(key, extent, deviation, most, split=(), dtype=jnp.bfloat16):
    gain = steps_of(key, extent, split, -0.22, 0.18) if split else 1.0
    values = jax.random.normal(key, extent, jnp.float32) * deviation * gain
    return jnp.minimum(jnp.maximum(values, -most), most).astype(dtype)


def setup_inputs(seed: int = 0) -> dict:
    arg_keys = jax.random.split(jax.random.key(seed), 9)
    return {
        "images": noise(arg_keys[0], (IMAGES, SIDE, SIDE, CIN), 1.0, 6.0, ((0, 256),)),
        "cotangent": noise(arg_keys[1], (IMAGES, SIDE, SIDE, CIN), 1.0, 6.0, ((0, 256),)),
        "w_first": noise(arg_keys[2], (REPLICAS, CIN, MID), 1.0, 6.0, ((0, 128), (1, 2)), jnp.float32),
        "w_middle": noise(arg_keys[3], (REPLICAS, 9 * MID, MID), 1.0, 6.0, ((0, 128), (1, 2)), jnp.float32),
        "w_last": noise(arg_keys[4], (REPLICAS, MID, CIN), 1.0, 6.0, ((0, 128), (2, 2)), jnp.float32),
        "m_first": noise(arg_keys[5], (REPLICAS, CIN, MID), 1.0, 6.0, ((0, 128), (1, 2)), jnp.float32),
        "m_middle": noise(arg_keys[6], (REPLICAS, 9 * MID, MID), 1.0, 6.0, ((0, 128), (1, 2)), jnp.float32),
        "m_last": noise(arg_keys[7], (REPLICAS, MID, CIN), 1.0, 6.0, ((0, 128), (2, 2)), jnp.float32),
    }


learn_rate = 0.1
momentum_coef = 0.9


def slope(value):
    sig = jax.nn.sigmoid(value)
    return sig * (1.0 + value * (1.0 - sig))


def block_grads(images, cotangent, e_first, e_middle, e_last):
    count, side, _, chans = images.shape
    mid = e_first.shape[1]
    rows = images.reshape(-1, chans)
    cot_rows = cotangent.reshape(-1, chans)
    h_first = jnp.dot(rows, e_first, preferred_element_type=jnp.float32)
    a_first = jax.nn.silu(h_first).astype(jnp.bfloat16)
    padded = jnp.pad(a_first.reshape(count, side, side, mid), ((0, 0), (1, 1), (1, 1), (0, 0)))
    slices = []
    for k_row in range(3):
        for k_col in range(3):
            slices.append(padded[:, k_row:k_row + side, k_col:k_col + side, :].reshape(-1, mid))
    h_middle = jnp.zeros((rows.shape[0], mid), jnp.float32)
    for k in range(9):
        h_middle = h_middle + jnp.dot(slices[k], e_middle[k * mid:(k + 1) * mid], preferred_element_type=jnp.float32)
    a_middle = jax.nn.silu(h_middle).astype(jnp.bfloat16)
    h_last = jnp.dot(a_middle, e_last, preferred_element_type=jnp.float32)
    pre_out = h_last + rows.astype(jnp.float32)
    d_last = (cot_rows.astype(jnp.float32) * slope(pre_out)).astype(jnp.bfloat16)
    g_last = jnp.einsum("rm,rc->mc", a_middle, d_last, preferred_element_type=jnp.float32)
    da_middle = jnp.einsum("rc,mc->rm", d_last, e_last, preferred_element_type=jnp.float32)
    d_middle = (da_middle * slope(h_middle)).astype(jnp.bfloat16)
    g_parts = []
    back_sum = jnp.zeros((count, side + 2, side + 2, mid), jnp.float32)
    for k in range(9):
        k_row, k_col = k // 3, k % 3
        g_parts.append(jnp.einsum("rm,rn->mn", slices[k], d_middle, preferred_element_type=jnp.float32))
        term = jnp.einsum("rn,mn->rm", d_middle, e_middle[k * mid:(k + 1) * mid], preferred_element_type=jnp.float32)
        term = term.reshape(count, side, side, mid)
        back_sum = back_sum + jnp.pad(term, ((0, 0), (k_row, 2 - k_row), (k_col, 2 - k_col), (0, 0)))
    g_middle = jnp.concatenate(g_parts, axis=0)
    da_first = back_sum[:, 1:-1, 1:-1, :].reshape(-1, mid)
    d_first = (da_first * slope(h_first)).astype(jnp.bfloat16)
    g_first = jnp.einsum("rc,rm->cm", rows, d_first, preferred_element_type=jnp.float32)
    return g_first, g_middle, g_last


def reference(images, cotangent, w_first, w_middle, w_last, m_first, m_middle, m_last):
    per_rep = N_DP * IMG_DEV
    imgs = images.reshape(N_GOSSIP, per_rep, SIDE, SIDE, CIN)
    cots = cotangent.reshape(N_GOSSIP, per_rep, SIDE, SIDE, CIN)
    scale_first = CIN ** -0.5
    scale_middle = (9 * MID) ** -0.5
    scale_last = MID ** -0.5
    weights = [w_first, w_middle, w_last]
    moments = [m_first, m_middle, m_last]
    scales = [scale_first, scale_middle, scale_last]
    for dist in (1, 2):
        def one_replica(items):
            x_rep, c_rep, wa, wb, wc = items
            return block_grads(x_rep, c_rep, (wa * scale_first).astype(jnp.bfloat16),
                               (wb * scale_middle).astype(jnp.bfloat16), (wc * scale_last).astype(jnp.bfloat16))

        grads = lax.map(one_replica, (imgs, cots, weights[0], weights[1], weights[2]))
        for idx in range(3):
            moments[idx] = momentum_coef * moments[idx] + scales[idx] * grads[idx]
            weights[idx] = weights[idx] - learn_rate * moments[idx]
        for idx in range(3):
            weights[idx] = 0.5 * (weights[idx] + jnp.roll(weights[idx], dist, axis=0))
            moments[idx] = 0.5 * (moments[idx] + jnp.roll(moments[idx], dist, axis=0))
    return (weights[0], weights[1], weights[2], moments[0], moments[1], moments[2])
```

```python
import functools

import jax
import jax.numpy as jnp
from jax import lax
from jax.experimental import pallas as pl
from jax.experimental.pallas import tpu as pltpu
from jax.sharding import PartitionSpec as P

CIN = 512
MID = 128
SIDE = 28
PITCH = 32
ROWS = SIDE * PITCH
BF16 = jnp.bfloat16
F32 = jnp.float32
MESH = pl.DeviceIdType.MESH
SCALES = (CIN ** (-0.5), (9 * MID) ** (-0.5), MID ** (-0.5))
SHARDS = ((256, 128), (576, 128), (128, 256))
FULLS = ((512, 128), (1152, 128), (128, 512))
learn_rate = 0.1
momentum_coef = 0.9

CHUNKS = ((0, 0, 256), (1, 0, 192), (1, 192, 192), (1, 384, 192), (2, 0, 128))
N_CHUNKS = len(CHUNKS)
E, W, G, M = range(4)


def sigmoid(v):
    return 0.5 * jnp.tanh(0.5 * v) + 0.5


def dot(a, b):
    return jnp.dot(a, b, preferred_element_type=F32)


def dot_nt(a, b):
    return lax.dot_general(a, b, (((1,), (1,)), ((), ())), preferred_element_type=F32)


def half(idx, ref, which, row, rows):
    if idx == 2:
        return ref.at[pl.ds(row, rows), pl.ds(pl.multiple_of(which * 256, 256), 256)]
    start = pl.multiple_of(which * SHARDS[idx][0] + row, 16)
    return ref.at[pl.ds(start, rows), :]


def pad_pixels(src, dst):
    dst[...] = jnp.zeros_like(dst)
    for i in range(SIDE):
        dst[pl.ds(i * PITCH, SIDE), :] = src[i]


def kernel(*refs):
    images, cotangent = refs[0:2]
    w_in, m_in = refs[2:5], refs[5:8]
    w_out, m_out = refs[8:11], refs[11:14]
    (
        x_raw, c_raw, x, xt, cot, e2f, e2r, a1s, d2s, a1t, a2, slope1, slope2, d3,
        w1, w2, w3, m1, m2, m3, g1, g2, g3,
        e1, e2, e3, wb1, wb2, wb3, wa1, wa2, wa3, gb1, gb2, gb3, ga1, ga2, ga3,
        mb1, mb2, mb3, ma1, ma2, ma3, send_sem, recv_sem, in_sem,
    ) = refs[14:]
    w, m, g, e = (w1, w2, w3), (m1, m2, m3), (g1, g2, g3), (e1, e2, e3)
    wb, wa, gb, ga, mb, ma = (
        (wb1, wb2, wb3), (wa1, wa2, wa3), (gb1, gb2, gb3), (ga1, ga2, ga3),
        (mb1, mb2, mb3), (ma1, ma2, ma3),
    )
    me, dp = lax.axis_index("gossip"), lax.axis_index("dp")
    count = lax.axis_size("gossip")

    def at(steps):
        return (lax.rem(me + steps + count, count), dp)

    partner = (me, 1 - dp)

    barrier = pltpu.get_barrier_semaphore()
    for other in (partner, at(1), at(-1), at(2), at(-2)):
        pl.semaphore_signal(barrier, inc=1, device_id=other, device_id_type=MESH)

    loads = {}
    for n, (src, dst) in enumerate(
        list(zip(w_in, w)) + [(images, x_raw), (cotangent, c_raw)] + list(zip(m_in, m))
    ):
        loads[n] = pltpu.make_async_copy(src, dst, in_sem.at[n])
        loads[n].start()

    def remote(kind, it, k):
        idx, row, rows = CHUNKS[k]
        rs = pl.ds(row, rows)
        if kind == E:
            src = half(idx, e[idx].at[it], dp, row, rows)
            dst, to = src, partner
        elif kind == W:
            src, dst, to = wb[idx].at[it, rs, :], wa[idx].at[it, rs, :], at(it + 1)
        elif kind == G:
            src, dst, to = gb[idx].at[it, rs, :], ga[idx].at[it, rs, :], partner
        else:
            src, dst, to = mb[idx].at[it, rs, :], ma[idx].at[it, rs, :], at(it + 1)
        return pltpu.make_async_remote_copy(
            src_ref=src, dst_ref=dst, send_sem=send_sem.at[kind, it, k],
            recv_sem=recv_sem.at[kind, it, k], device_id=to, device_id_type=MESH,
        )

    def of(idx):
        return [k for k in range(N_CHUNKS) if CHUNKS[k][0] == idx]

    for idx in range(3):
        loads[idx].wait()
        full = (0, SHARDS[idx][0])
        half(idx, e[idx].at[0], dp, *full)[...] = (w[idx][...] * SCALES[idx]).astype(BF16)
        wb[idx][0] = w[idx][...].astype(BF16)
    pl.semaphore_wait(barrier, 5)
    for k in range(N_CHUNKS):
        remote(E, 0, k).start()

    d2s[...] = jnp.zeros_like(d2s)
    loads[3].wait()
    pad_pixels(x_raw, x)
    xt[...] = x[...].T
    loads[4].wait()
    pad_pixels(c_raw, cot)
    for n in range(5, 8):
        loads[n].wait()

    zero = jnp.zeros((PITCH, MID), F32)

    def take(it, k):
        idx, row, rows = CHUNKS[k]
        rs = pl.ds(row, rows)
        remote(G, it, k).wait_recv()
        total = half(idx, g[idx], dp, row, rows)[...] + ga[idx][it, rs, :].astype(F32)
        new = momentum_coef * m[idx][rs, :] + SCALES[idx] * total
        m[idx][rs, :] = new
        mb[idx][it, rs, :] = new.astype(BF16)
        remote(M, it, k).start()

    def mix(it, k):
        idx, row, rows = CHUNKS[k]
        rs = pl.ds(row, rows)
        remote(M, it, k).wait_recv()
        mean = 0.5 * (m[idx][rs, :] + ma[idx][it, rs, :].astype(F32))
        if it == 0:
            remote(W, it, k).wait_recv()
        weight = 0.5 * (w[idx][rs, :] + wa[idx][it, rs, :].astype(F32)) - learn_rate * mean
        if it == 0:
            m[idx][rs, :] = mean
            w[idx][rs, :] = weight
            half(idx, e[idx].at[1], dp, row, rows)[...] = (weight * SCALES[idx]).astype(BF16)
            remote(E, 1, k).start()
            wb[idx][1, rs, :] = weight.astype(BF16)
            remote(W, 1, k).start()
        else:
            m_out[idx][rs, :] = mean
            w_out[idx][rs, :] = weight

    def send_grad(it, idx):
        for k in of(idx):
            _, row, rows = CHUNKS[k]
            gb[idx][it, pl.ds(row, rows), :] = half(idx, g[idx], 1 - dp, row, rows)[...].astype(BF16)
            remote(G, it, k).start()

    for it in range(2):
        for k in of(0):
            remote(E, it, k).wait_recv()
        h1 = dot(x[...], e1[it])
        sig = sigmoid(h1)
        act1 = h1 * sig
        slope1[...] = sig * (1.0 + h1 * (1.0 - sig))
        a1s[:, 0:128] = pltpu.roll(act1, 1, 0).astype(BF16)
        a1s[:, 128:256] = act1.astype(BF16)
        a1s[:, 256:384] = pltpu.roll(act1, ROWS - 1, 0).astype(BF16)
        a1t[...] = act1.astype(BF16).T
        for k in of(1):
            remote(E, it, k).wait_recv()
        for ky in range(3):
            e2f[:, ky * 128 : (ky + 1) * 128] = e2[it, pl.ds(ky * 384, 384), :]
            for kx in range(3):
                e2r[pl.ds(ky * 128, 128), kx * 128 : (kx + 1) * 128] = e2[
                    it, pl.ds((3 * ky + kx) * 128, 128), :
                ]
        u = dot(a1s[...], e2f[...])
        h2 = (
            u[:, 128:256]
            + jnp.concatenate([zero, u[: ROWS - PITCH, 0:128]], axis=0)
            + jnp.concatenate([u[PITCH:, 256:384], zero], axis=0)
        )
        sig = sigmoid(h2)
        slope2[...] = sig * (1.0 + h2 * (1.0 - sig))
        a2[...] = (h2 * sig).astype(BF16)
        for k in of(2):
            remote(E, it, k).wait_recv()
        if it == 0:
            for k in range(N_CHUNKS):
                remote(W, 0, k).start()
        for j in range(7):
            rs = pl.ds(j * 128, 128)
            pre = dot(a2[rs, :], e3[it]) + x[rs, :].astype(F32)
            sig = sigmoid(pre)
            d3[rs, :] = (cot[rs, :].astype(F32) * (sig * (1.0 + pre * (1.0 - sig)))).astype(BF16)
        if it == 1:
            g3[...] = dot(a2[...].T, d3[...])
            send_grad(it, 2)
        d2 = dot_nt(d3[...], e3[it]) * slope2[...]
        inner = pl.ds(PITCH, ROWS)
        d2s[inner, 0:128] = pltpu.roll(d2, ROWS - 1, 0).astype(BF16)
        d2s[inner, 128:256] = d2.astype(BF16)
        d2s[inner, 256:384] = pltpu.roll(d2, 1, 0).astype(BF16)

        def first():
            t = dot_nt(d2s[inner, :], e2r[...])
            da1 = (
                t[:, 128:256]
                + jnp.concatenate([t[PITCH:, 0:128], zero], axis=0)
                + jnp.concatenate([zero, t[: ROWS - PITCH, 256:384]], axis=0)
            )
            d1 = (da1 * slope1[...]).astype(BF16)
            g1[...] = dot(xt[...], d1)
            send_grad(it, 0)

        def middle():
            for ky in range(3):
                gk = dot(a1t[...], d2s[pl.ds((2 - ky) * PITCH, ROWS), :])
                for kx in range(3):
                    g2[pl.ds((3 * ky + kx) * 128, 128), :] = gk[:, kx * 128 : (kx + 1) * 128]
            send_grad(it, 1)

        if it == 0:
            first()
            middle()
            g3[...] = dot(a2[...].T, d3[...])
            send_grad(it, 2)
            order = (0, 1, 2, 3, 4)
        else:
            middle()
            first()
            for k in range(N_CHUNKS):
                remote(W, 1, k).wait_recv()
            order = (4, 1, 2, 3, 0)
        lag = 3
        for n in range(N_CHUNKS + lag):
            if n < N_CHUNKS:
                take(it, order[n])
            if n >= lag:
                mix(it, order[n - lag])

    for it in range(2):
        for kind in range(4):
            for k in range(N_CHUNKS):
                remote(kind, it, k).wait_send()


def body(images, cotangent, *state):
    vmem = pl.BlockSpec(memory_space=pltpu.VMEM)
    hbm = pl.BlockSpec(memory_space=pl.ANY)
    pix = (SIDE, SIDE, CIN)
    pair = [pltpu.VMEM((2,) + s, BF16) for s in SHARDS]
    outs = pl.pallas_call(
        kernel,
        out_shape=[jax.ShapeDtypeStruct(s, F32) for s in SHARDS * 2],
        in_specs=[hbm] * 8,
        out_specs=[vmem] * 6,
        scratch_shapes=[
            pltpu.VMEM(pix, BF16), pltpu.VMEM(pix, BF16),
            pltpu.VMEM((ROWS, CIN), BF16), pltpu.VMEM((CIN, ROWS), BF16), pltpu.VMEM((ROWS, CIN), BF16),
            pltpu.VMEM((384, 384), BF16), pltpu.VMEM((384, 384), BF16),
            pltpu.VMEM((ROWS, 384), BF16), pltpu.VMEM((ROWS + 2 * PITCH, 384), BF16),
            pltpu.VMEM((MID, ROWS), BF16), pltpu.VMEM((ROWS, MID), BF16),
            pltpu.VMEM((ROWS, MID), F32), pltpu.VMEM((ROWS, MID), F32),
            pltpu.VMEM((ROWS, CIN), BF16),
        ]
        + [pltpu.VMEM(s, F32) for s in SHARDS] * 2
        + [pltpu.VMEM(s, F32) for s in FULLS]
        + [pltpu.VMEM((2,) + s, BF16) for s in FULLS]
        + pair * 6
        + [
            pltpu.SemaphoreType.DMA((4, 2, N_CHUNKS)),
            pltpu.SemaphoreType.DMA((4, 2, N_CHUNKS)),
            pltpu.SemaphoreType.DMA((8,)),
        ],
        compiler_params=pltpu.CompilerParams(
            collective_id=0, has_side_effects=True, vmem_limit_bytes=56 << 20
        ),
    )(images[0], cotangent[0], *[s[0] for s in state])
    return tuple(o[None] for o in outs)


def solution(mesh):
    pixels = P(("gossip", "dp"), None, None, None)
    rows, columns = P("gossip", "dp", None), P("gossip", None, "dp")
    return jax.shard_map(
        body,
        mesh=mesh,
        in_specs=(pixels, pixels) + (rows, rows, columns) * 2,
        out_specs=(rows, rows, columns) * 2,
        check_vma=False,
    )
```

```python
import functools

import jax
import jax.numpy as jnp
from jax import lax
from jax.experimental import pallas as pl
from jax.experimental.pallas import tpu as pltpu
from jax.sharding import PartitionSpec as P

CIN = 512
MID = 128
SIDE = 28
PITCH = 32
ROWS = SIDE * PITCH
BF16 = jnp.bfloat16
F32 = jnp.float32
MESH = pl.DeviceIdType.MESH
SCALES = (CIN ** (-0.5), (9 * MID) ** (-0.5), MID ** (-0.5))
SHARDS = ((256, 128), (576, 128), (128, 256))
FULLS = ((512, 128), (1152, 128), (128, 512))
learn_rate = 0.1
momentum_coef = 0.9

CHUNKS = ((0, 0, 256), (1, 0, 192), (1, 192, 192), (1, 384, 192), (2, 0, 128))
N_CHUNKS = len(CHUNKS)
E, W, G, M = range(4)
ROUTES = {
    (W, 0): {0: 1, 1: 1, 2: 2, 3: 2, 4: 0},
    (W, 1): {0: 1, 1: 1, 2: 2, 3: 2, 4: 0},
    (M, 0): {0: 1, 1: 2, 2: 2},
    (M, 1): {4: 1, 1: 2, 2: 0},
}


def sigmoid(v):
    return 0.5 * jnp.tanh(0.5 * v) + 0.5


def dot(a, b):
    return jnp.dot(a, b, preferred_element_type=F32)


def dot_nt(a, b):
    return lax.dot_general(a, b, (((1,), (1,)), ((), ())), preferred_element_type=F32)


def half(idx, ref, which, row, rows):
    if idx == 2:
        return ref.at[pl.ds(row, rows), pl.ds(pl.multiple_of(which * 256, 256), 256)]
    start = pl.multiple_of(which * SHARDS[idx][0] + row, 16)
    return ref.at[pl.ds(start, rows), :]


def pad_pixels(src, dst):
    dst[...] = jnp.zeros_like(dst)
    for i in range(SIDE):
        dst[pl.ds(i * PITCH, SIDE), :] = src[i]


def kernel(*refs):
    images, cotangent = refs[0:2]
    w_in, m_in = refs[2:5], refs[5:8]
    w_out, m_out = refs[8:11], refs[11:14]
    (
        x_raw, c_raw, x, xt, cot, e2f, e2r, a1s, d2s, a1t, a2, slope1, slope2, d3,
        w1, w2, w3, m1, m2, m3, g1, g2, g3,
        e1, e2, e3, wb1, wb2, wb3, wa1, wa2, wa3, gb1, gb2, gb3, ga1, ga2, ga3,
        mb1, mb2, mb3, ma1, ma2, ma3,
        rw1, rw2, rw3, rm1, rm2, rm3, send_sem, recv_sem, in_sem, relay_send, relay_recv,
    ) = refs[14:]
    w, m, g, e = (w1, w2, w3), (m1, m2, m3), (g1, g2, g3), (e1, e2, e3)
    wb, wa, gb, ga, mb, ma = (
        (wb1, wb2, wb3), (wa1, wa2, wa3), (gb1, gb2, gb3), (ga1, ga2, ga3),
        (mb1, mb2, mb3), (ma1, ma2, ma3),
    )
    me, dp = lax.axis_index("gossip"), lax.axis_index("dp")
    count = lax.axis_size("gossip")

    def at(steps):
        return (lax.rem(me + steps + count, count), dp)

    partner = (me, 1 - dp)
    core, spot = lax.rem(me, 2), lax.rem(me, 64) // 2
    x_lo = me // 64
    far = 64 * (1 - x_lo)
    last, origin = spot == 31, spot == 0
    relays = (spot == 7) | (spot == 15) | (spot == 23)
    relay_bufs = {W: (rw1, rw2, rw3), M: (rm1, rm2, rm3)}

    barrier = pltpu.get_barrier_semaphore()
    for other in (partner, at(1), at(-1), at(2), at(-2)):
        pl.semaphore_signal(barrier, inc=1, device_id=other, device_id_type=MESH)

    def greet(other):
        pl.semaphore_signal(barrier, inc=1, device_id=(other, dp), device_id_type=MESH)

    @pl.when(last)
    def _():
        for y in range(3):
            greet(64 * x_lo + 16 * y + 14 + core)

    @pl.when(relays)
    def _():
        greet(64 * x_lo + 62 + core)
        greet(far + core)

        @pl.when(core == 1)
        def _():
            greet(far)

    @pl.when(origin)
    def _():
        for y in range(3):
            greet(far + 16 * y + 14 + core)

            @pl.when(core == 0)
            def _():
                greet(far + 16 * y + 15)

    guests = 5 + jnp.where(last, 3, 0) + jnp.where(relays, 2 + core, 0) + jnp.where(origin, 6 - 3 * core, 0)
    loads = {}
    for n, (src, dst) in enumerate(
        list(zip(w_in, w)) + [(images, x_raw), (cotangent, c_raw)] + list(zip(m_in, m))
    ):
        loads[n] = pltpu.make_async_copy(src, dst, in_sem.at[n])
        loads[n].start()

    def remote(kind, it, k):
        idx, row, rows = CHUNKS[k]
        rs = pl.ds(row, rows)
        if kind == E:
            src = half(idx, e[idx].at[it], dp, row, rows)
            dst, to = src, partner
        elif kind == W:
            src, dst, to = wb[idx].at[it, rs, :], wa[idx].at[it, rs, :], at(it + 1)
        elif kind == G:
            src, dst, to = gb[idx].at[it, rs, :], ga[idx].at[it, rs, :], partner
        else:
            src, dst, to = mb[idx].at[it, rs, :], ma[idx].at[it, rs, :], at(it + 1)
        return pltpu.make_async_remote_copy(
            src_ref=src, dst_ref=dst, send_sem=send_sem.at[kind, it, k],
            recv_sem=recv_sem.at[kind, it, k], device_id=to, device_id_type=MESH,
        )

    def to_relay(kind, it, k):
        idx, row, rows = CHUNKS[k]
        rs = pl.ds(row, rows)
        src = {W: wb, M: mb}[kind][idx].at[it, rs, :]
        y = ROUTES[kind, it][k]
        return pltpu.make_async_remote_copy(
            src_ref=src, dst_ref=relay_bufs[kind][idx].at[it, rs, :],
            send_sem=send_sem.at[kind, it, k], recv_sem=relay_recv.at[kind // 2, it, k],
            device_id=(64 * x_lo + 16 * y + 14 + core, dp), device_id_type=MESH,
        )

    def from_relay(kind, it, k):
        idx, row, rows = CHUNKS[k]
        rs = pl.ds(row, rows)
        return pltpu.make_async_remote_copy(
            src_ref=relay_bufs[kind][idx].at[it, rs, :], dst_ref={W: wa, M: ma}[kind][idx].at[it, rs, :],
            send_sem=relay_send.at[kind // 2, it, k], recv_sem=recv_sem.at[kind, it, k],
            device_id=(far + it * core, dp), device_id_type=MESH,
        )

    def active(it, where):
        return where if it == 1 else where & (core == 1)

    def gossip(kind, it, k):
        if k not in ROUTES[kind, it]:
            remote(kind, it, k).start()
            return
        cross = active(it, last)

        @pl.when(cross)
        def _():
            to_relay(kind, it, k).start()

        @pl.when(jnp.logical_not(cross))
        def _():
            remote(kind, it, k).start()

    def relay(kind, it, chunks, done=False):
        for y in range(3):
            mine = [k for k in chunks if ROUTES[kind, it].get(k) == y]
            if mine:

                @pl.when(active(it, spot == 8 * y + 7))
                def _():
                    for k in mine:
                        if done:
                            from_relay(kind, it, k).wait_send()
                        else:
                            to_relay(kind, it, k).wait_recv()
                            from_relay(kind, it, k).start()

    def of(idx):
        return [k for k in range(N_CHUNKS) if CHUNKS[k][0] == idx]

    for idx in range(3):
        loads[idx].wait()
        full = (0, SHARDS[idx][0])
        half(idx, e[idx].at[0], dp, *full)[...] = (w[idx][...] * SCALES[idx]).astype(BF16)
        wb[idx][0] = w[idx][...].astype(BF16)
    pl.semaphore_wait(barrier, guests)
    for k in range(N_CHUNKS):
        remote(E, 0, k).start()
    for k in range(N_CHUNKS):
        gossip(W, 0, k)

    d2s[...] = jnp.zeros_like(d2s)
    loads[3].wait()
    pad_pixels(x_raw, x)
    xt[...] = x[...].T
    loads[4].wait()
    pad_pixels(c_raw, cot)
    for n in range(5, 8):
        loads[n].wait()

    zero = jnp.zeros((PITCH, MID), F32)

    def take(it, k):
        idx, row, rows = CHUNKS[k]
        rs = pl.ds(row, rows)
        remote(G, it, k).wait_recv()
        total = half(idx, g[idx], dp, row, rows)[...] + ga[idx][it, rs, :].astype(F32)
        new = momentum_coef * m[idx][rs, :] + SCALES[idx] * total
        m[idx][rs, :] = new
        mb[idx][it, rs, :] = new.astype(BF16)
        gossip(M, it, k)

    def mix(it, k):
        idx, row, rows = CHUNKS[k]
        rs = pl.ds(row, rows)
        remote(M, it, k).wait_recv()
        mean = 0.5 * (m[idx][rs, :] + ma[idx][it, rs, :].astype(F32))
        if it == 0:
            remote(W, it, k).wait_recv()
        weight = 0.5 * (w[idx][rs, :] + wa[idx][it, rs, :].astype(F32)) - learn_rate * mean
        if it == 0:
            m[idx][rs, :] = mean
            w[idx][rs, :] = weight
            half(idx, e[idx].at[1], dp, row, rows)[...] = (weight * SCALES[idx]).astype(BF16)
            remote(E, 1, k).start()
            wb[idx][1, rs, :] = weight.astype(BF16)
            gossip(W, 1, k)
        else:
            m_out[idx][rs, :] = mean
            w_out[idx][rs, :] = weight

    def send_grad(it, idx):
        for k in of(idx):
            _, row, rows = CHUNKS[k]
            gb[idx][it, pl.ds(row, rows), :] = half(idx, g[idx], 1 - dp, row, rows)[...].astype(BF16)
            remote(G, it, k).start()

    for it in range(2):
        for k in of(0):
            remote(E, it, k).wait_recv()
        h1 = dot(x[...], e1[it])
        sig = sigmoid(h1)
        act1 = h1 * sig
        slope1[...] = sig * (1.0 + h1 * (1.0 - sig))
        a1s[:, 0:128] = pltpu.roll(act1, 1, 0).astype(BF16)
        a1s[:, 128:256] = act1.astype(BF16)
        a1s[:, 256:384] = pltpu.roll(act1, ROWS - 1, 0).astype(BF16)
        a1t[...] = act1.astype(BF16).T
        for k in of(1):
            remote(E, it, k).wait_recv()
        for ky in range(3):
            e2f[:, ky * 128 : (ky + 1) * 128] = e2[it, pl.ds(ky * 384, 384), :]
            for kx in range(3):
                e2r[pl.ds(ky * 128, 128), kx * 128 : (kx + 1) * 128] = e2[
                    it, pl.ds((3 * ky + kx) * 128, 128), :
                ]
        u = dot(a1s[...], e2f[...])
        h2 = (
            u[:, 128:256]
            + jnp.concatenate([zero, u[: ROWS - PITCH, 0:128]], axis=0)
            + jnp.concatenate([u[PITCH:, 256:384], zero], axis=0)
        )
        sig = sigmoid(h2)
        slope2[...] = sig * (1.0 + h2 * (1.0 - sig))
        a2[...] = (h2 * sig).astype(BF16)
        for k in of(2):
            remote(E, it, k).wait_recv()
        relay(W, it, range(N_CHUNKS))
        for j in range(7):
            rs = pl.ds(j * 128, 128)
            pre = dot(a2[rs, :], e3[it]) + x[rs, :].astype(F32)
            sig = sigmoid(pre)
            d3[rs, :] = (cot[rs, :].astype(F32) * (sig * (1.0 + pre * (1.0 - sig)))).astype(BF16)
        if it == 1:
            g3[...] = dot(a2[...].T, d3[...])
            send_grad(it, 2)
        d2 = dot_nt(d3[...], e3[it]) * slope2[...]
        inner = pl.ds(PITCH, ROWS)
        d2s[inner, 0:128] = pltpu.roll(d2, ROWS - 1, 0).astype(BF16)
        d2s[inner, 128:256] = d2.astype(BF16)
        d2s[inner, 256:384] = pltpu.roll(d2, 1, 0).astype(BF16)

        def first():
            t = dot_nt(d2s[inner, :], e2r[...])
            da1 = (
                t[:, 128:256]
                + jnp.concatenate([t[PITCH:, 0:128], zero], axis=0)
                + jnp.concatenate([zero, t[: ROWS - PITCH, 256:384]], axis=0)
            )
            d1 = (da1 * slope1[...]).astype(BF16)
            g1[...] = dot(xt[...], d1)
            send_grad(it, 0)

        def middle():
            for ky in range(3):
                gk = dot(a1t[...], d2s[pl.ds((2 - ky) * PITCH, ROWS), :])
                for kx in range(3):
                    g2[pl.ds((3 * ky + kx) * 128, 128), :] = gk[:, kx * 128 : (kx + 1) * 128]
            send_grad(it, 1)

        if it == 0:
            first()
            middle()
            g3[...] = dot(a2[...].T, d3[...])
            send_grad(it, 2)
            order = (0, 1, 2, 3, 4)
        else:
            middle()
            first()
            for k in range(N_CHUNKS):
                remote(W, 1, k).wait_recv()
            order = (4, 1, 2, 3, 0)
        lag = 3
        for n in range(N_CHUNKS + lag):
            if n < N_CHUNKS:
                take(it, order[n])
            if n >= lag:
                relay(M, it, (order[n - lag],))
                mix(it, order[n - lag])

    for it in range(2):
        for kind in range(4):
            for k in range(N_CHUNKS):
                remote(kind, it, k).wait_send()
        for kind in (W, M):
            relay(kind, it, range(N_CHUNKS), done=True)


def write_out(*refs):
    copies = [pltpu.make_async_copy(refs[i], refs[6 + i], refs[12].at[i]) for i in range(6)]
    for c in copies:
        c.start()
    for c in copies:
        c.wait()


def body(images, cotangent, *state):
    vmem = pl.BlockSpec(memory_space=pltpu.VMEM)
    hbm = pl.BlockSpec(memory_space=pl.ANY)
    pix = (SIDE, SIDE, CIN)
    pair = [pltpu.VMEM((2,) + s, BF16) for s in SHARDS]
    outs = pl.pallas_call(
        kernel,
        out_shape=[jax.ShapeDtypeStruct(s, F32) for s in SHARDS * 2],
        in_specs=[hbm] * 8,
        out_specs=[vmem] * 6,
        scratch_shapes=[
            pltpu.VMEM(pix, BF16), pltpu.VMEM(pix, BF16),
            pltpu.VMEM((ROWS, CIN), BF16), pltpu.VMEM((CIN, ROWS), BF16), pltpu.VMEM((ROWS, CIN), BF16),
            pltpu.VMEM((384, 384), BF16), pltpu.VMEM((384, 384), BF16),
            pltpu.VMEM((ROWS, 384), BF16), pltpu.VMEM((ROWS + 2 * PITCH, 384), BF16),
            pltpu.VMEM((MID, ROWS), BF16), pltpu.VMEM((ROWS, MID), BF16),
            pltpu.VMEM((ROWS, MID), F32), pltpu.VMEM((ROWS, MID), F32),
            pltpu.VMEM((ROWS, CIN), BF16),
        ]
        + [pltpu.VMEM(s, F32) for s in SHARDS] * 2
        + [pltpu.VMEM(s, F32) for s in FULLS]
        + [pltpu.VMEM((2,) + s, BF16) for s in FULLS]
        + pair * 8
        + [
            pltpu.SemaphoreType.DMA((4, 2, N_CHUNKS)),
            pltpu.SemaphoreType.DMA((4, 2, N_CHUNKS)),
            pltpu.SemaphoreType.DMA((8,)),
            pltpu.SemaphoreType.DMA((2, 2, N_CHUNKS)),
            pltpu.SemaphoreType.DMA((2, 2, N_CHUNKS)),
        ],
        compiler_params=pltpu.CompilerParams(
            collective_id=0, has_side_effects=True, vmem_limit_bytes=56 << 20
        ),
    )(images[0], cotangent[0], *[s[0] for s in state])
    outs = pl.pallas_call(
        write_out,
        out_shape=[jax.ShapeDtypeStruct(s, F32) for s in SHARDS * 2],
        in_specs=[pl.BlockSpec(memory_space=pltpu.VMEM)] * 6,
        out_specs=[pl.BlockSpec(memory_space=pltpu.HBM)] * 6,
        scratch_shapes=[pltpu.SemaphoreType.DMA((6,))],
    )(*outs)
    return tuple(o[None] for o in outs)


def solution(mesh):
    pixels = P(("gossip", "dp"), None, None, None)
    rows, columns = P("gossip", "dp", None), P("gossip", None, "dp")
    return jax.shard_map(
        body,
        mesh=mesh,
        in_specs=(pixels, pixels) + (rows, rows, columns) * 2,
        out_specs=(rows, rows, columns) * 2,
        check_vma=False,
    )
```

```python
import functools

import jax
import jax.numpy as jnp
from jax import lax
from jax.experimental import pallas as pl
from jax.experimental.pallas import tpu as pltpu
from jax.sharding import PartitionSpec as P

CIN = 512
MID = 128
SIDE = 28
PITCH = 32
ROWS = SIDE * PITCH
BF16 = jnp.bfloat16
F32 = jnp.float32
MESH = pl.DeviceIdType.MESH
SCALES = (CIN ** (-0.5), (9 * MID) ** (-0.5), MID ** (-0.5))
SHARDS = ((256, 128), (576, 128), (128, 256))
FULLS = ((512, 128), (1152, 128), (128, 512))
learn_rate = 0.1
momentum_coef = 0.9

CHUNKS = ((0, 0, 256), (1, 0, 192), (1, 192, 192), (1, 384, 192), (2, 0, 128))
N_CHUNKS = len(CHUNKS)
E, W, G, M = range(4)
ROUTES = {
    (W, 0): {0: 1, 1: 1, 2: 2, 3: 2, 4: 0},
    (W, 1): {0: 1, 1: 1, 2: 2, 3: 2, 4: 0},
    (M, 0): {3: 2, 4: 1},
    (M, 1): {4: 1, 1: 2, 2: 0},
}


def sigmoid(v):
    return 0.5 * jnp.tanh(0.5 * v) + 0.5


def dot(a, b):
    return jnp.dot(a, b, preferred_element_type=F32)


def dot_nt(a, b):
    return lax.dot_general(a, b, (((1,), (1,)), ((), ())), preferred_element_type=F32)


def half(idx, ref, which, row, rows):
    if idx == 2:
        return ref.at[pl.ds(row, rows), pl.ds(pl.multiple_of(which * 256, 256), 256)]
    start = pl.multiple_of(which * SHARDS[idx][0] + row, 16)
    return ref.at[pl.ds(start, rows), :]


def pad_pixels(src, dst):
    dst[...] = jnp.zeros_like(dst)
    for i in range(SIDE):
        dst[pl.ds(i * PITCH, SIDE), :] = src[i]


def kernel(*refs):
    images, cotangent = refs[0:2]
    w_in, m_in = refs[2:5], refs[5:8]
    w_out, m_out = refs[8:11], refs[11:14]
    (
        x_raw, c_raw, x, xt, cot, e2f, e2r, a1s, d2s, a1t, a2, slope1, slope2, d3,
        w1, w2, w3, m1, m2, m3, g1, g2, g3,
        e1, e2, e3, wb1, wb2, wb3, wa1, wa2, wa3, gb1, gb2, gb3, ga1, ga2, ga3,
        mb1, mb2, mb3, ma1, ma2, ma3,
        rw1, rw2, rw3, rm1, rm2, rm3, send_sem, recv_sem, in_sem, relay_send, relay_recv,
    ) = refs[14:]
    w, m, g, e = (w1, w2, w3), (m1, m2, m3), (g1, g2, g3), (e1, e2, e3)
    wb, wa, gb, ga, mb, ma = (
        (wb1, wb2, wb3), (wa1, wa2, wa3), (gb1, gb2, gb3), (ga1, ga2, ga3),
        (mb1, mb2, mb3), (ma1, ma2, ma3),
    )
    me, dp = lax.axis_index("gossip"), lax.axis_index("dp")
    count = lax.axis_size("gossip")

    def at(steps):
        return (lax.rem(me + steps + count, count), dp)

    partner = (me, 1 - dp)
    core, spot = lax.rem(me, 2), lax.rem(me, 64) // 2
    x_lo = me // 64
    far = 64 * (1 - x_lo)
    last, origin = spot == 31, spot == 0
    relays = (spot == 7) | (spot == 15) | (spot == 23)
    relay_bufs = {W: (rw1, rw2, rw3), M: (rm1, rm2, rm3)}

    barrier = pltpu.get_barrier_semaphore()
    for other in (partner, at(1), at(-1), at(2), at(-2)):
        pl.semaphore_signal(barrier, inc=1, device_id=other, device_id_type=MESH)

    def greet(other):
        pl.semaphore_signal(barrier, inc=1, device_id=(other, dp), device_id_type=MESH)

    @pl.when(last)
    def _():
        for y in range(3):
            greet(64 * x_lo + 16 * y + 14 + core)

    @pl.when(relays)
    def _():
        greet(64 * x_lo + 62 + core)
        greet(far + core)

        @pl.when(core == 1)
        def _():
            greet(far)

    @pl.when(origin)
    def _():
        for y in range(3):
            greet(far + 16 * y + 14 + core)

            @pl.when(core == 0)
            def _():
                greet(far + 16 * y + 15)

    guests = 5 + jnp.where(last, 3, 0) + jnp.where(relays, 2 + core, 0) + jnp.where(origin, 6 - 3 * core, 0)
    loads = {}
    for n, (src, dst) in enumerate(
        list(zip(w_in, w)) + [(images, x_raw), (cotangent, c_raw)] + list(zip(m_in, m))
    ):
        loads[n] = pltpu.make_async_copy(src, dst, in_sem.at[n])
        loads[n].start()

    def remote(kind, it, k):
        idx, row, rows = CHUNKS[k]
        rs = pl.ds(row, rows)
        if kind == E:
            src = half(idx, e[idx].at[it], dp, row, rows)
            dst, to = src, partner
        elif kind == W:
            src, dst, to = wb[idx].at[it, rs, :], wa[idx].at[it, rs, :], at(it + 1)
        elif kind == G:
            src, dst, to = gb[idx].at[it, rs, :], ga[idx].at[it, rs, :], partner
        else:
            src, dst, to = mb[idx].at[it, rs, :], ma[idx].at[it, rs, :], at(it + 1)
        return pltpu.make_async_remote_copy(
            src_ref=src, dst_ref=dst, send_sem=send_sem.at[kind, it, k],
            recv_sem=recv_sem.at[kind, it, k], device_id=to, device_id_type=MESH,
        )

    def to_relay(kind, it, k):
        idx, row, rows = CHUNKS[k]
        rs = pl.ds(row, rows)
        src = {W: wb, M: mb}[kind][idx].at[it, rs, :]
        y = ROUTES[kind, it][k]
        return pltpu.make_async_remote_copy(
            src_ref=src, dst_ref=relay_bufs[kind][idx].at[it, rs, :],
            send_sem=send_sem.at[kind, it, k], recv_sem=relay_recv.at[kind // 2, it, k],
            device_id=(64 * x_lo + 16 * y + 14 + core, dp), device_id_type=MESH,
        )

    def from_relay(kind, it, k):
        idx, row, rows = CHUNKS[k]
        rs = pl.ds(row, rows)
        return pltpu.make_async_remote_copy(
            src_ref=relay_bufs[kind][idx].at[it, rs, :], dst_ref={W: wa, M: ma}[kind][idx].at[it, rs, :],
            send_sem=relay_send.at[kind // 2, it, k], recv_sem=recv_sem.at[kind, it, k],
            device_id=(far + it * core, dp), device_id_type=MESH,
        )

    def active(it, where):
        return where if it == 1 else where & (core == 1)

    def gossip(kind, it, k):
        if k not in ROUTES[kind, it]:
            remote(kind, it, k).start()
            return
        cross = active(it, last)

        @pl.when(cross)
        def _():
            to_relay(kind, it, k).start()

        @pl.when(jnp.logical_not(cross))
        def _():
            remote(kind, it, k).start()

    def relay(kind, it, chunks, done=False):
        for y in range(3):
            mine = [k for k in chunks if ROUTES[kind, it].get(k) == y]
            if mine:

                @pl.when(active(it, spot == 8 * y + 7))
                def _():
                    for k in mine:
                        if done:
                            from_relay(kind, it, k).wait_send()
                        else:
                            to_relay(kind, it, k).wait_recv()
                            from_relay(kind, it, k).start()

    def of(idx):
        return [k for k in range(N_CHUNKS) if CHUNKS[k][0] == idx]

    for idx in range(3):
        loads[idx].wait()
        full = (0, SHARDS[idx][0])
        half(idx, e[idx].at[0], dp, *full)[...] = (w[idx][...] * SCALES[idx]).astype(BF16)
        wb[idx][0] = w[idx][...].astype(BF16)
    pl.semaphore_wait(barrier, guests)
    for k in range(N_CHUNKS):
        remote(E, 0, k).start()
    for k in range(N_CHUNKS):
        gossip(W, 0, k)

    d2s[...] = jnp.zeros_like(d2s)
    loads[3].wait()
    pad_pixels(x_raw, x)
    xt[...] = x[...].T
    loads[4].wait()
    pad_pixels(c_raw, cot)
    for n in range(5, 8):
        loads[n].wait()

    zero = jnp.zeros((PITCH, MID), F32)

    def take(it, k):
        idx, row, rows = CHUNKS[k]
        rs = pl.ds(row, rows)
        remote(G, it, k).wait_recv()
        total = half(idx, g[idx], dp, row, rows)[...] + ga[idx][it, rs, :].astype(F32)
        new = momentum_coef * m[idx][rs, :] + SCALES[idx] * total
        m[idx][rs, :] = new
        mb[idx][it, rs, :] = new.astype(BF16)
        gossip(M, it, k)

    def mix(it, k):
        idx, row, rows = CHUNKS[k]
        rs = pl.ds(row, rows)
        remote(M, it, k).wait_recv()
        mean = 0.5 * (m[idx][rs, :] + ma[idx][it, rs, :].astype(F32))
        if it == 0:
            remote(W, it, k).wait_recv()
        weight = 0.5 * (w[idx][rs, :] + wa[idx][it, rs, :].astype(F32)) - learn_rate * mean
        if it == 0:
            m[idx][rs, :] = mean
            w[idx][rs, :] = weight
            half(idx, e[idx].at[1], dp, row, rows)[...] = (weight * SCALES[idx]).astype(BF16)
            remote(E, 1, k).start()
            wb[idx][1, rs, :] = weight.astype(BF16)
            gossip(W, 1, k)
        else:
            m_out[idx][rs, :] = mean
            w_out[idx][rs, :] = weight

    def send_grad(it, idx):
        for k in of(idx):
            _, row, rows = CHUNKS[k]
            gb[idx][it, pl.ds(row, rows), :] = half(idx, g[idx], 1 - dp, row, rows)[...].astype(BF16)
            remote(G, it, k).start()

    for it in range(2):
        for k in of(0):
            remote(E, it, k).wait_recv()
        h1 = dot(x[...], e1[it])
        sig = sigmoid(h1)
        act1 = h1 * sig
        slope1[...] = sig * (1.0 + h1 * (1.0 - sig))
        a1s[:, 0:128] = pltpu.roll(act1, 1, 0).astype(BF16)
        a1s[:, 128:256] = act1.astype(BF16)
        a1s[:, 256:384] = pltpu.roll(act1, ROWS - 1, 0).astype(BF16)
        a1t[...] = act1.astype(BF16).T
        for k in of(1):
            remote(E, it, k).wait_recv()
        for ky in range(3):
            e2f[:, ky * 128 : (ky + 1) * 128] = e2[it, pl.ds(ky * 384, 384), :]
            for kx in range(3):
                e2r[pl.ds(ky * 128, 128), kx * 128 : (kx + 1) * 128] = e2[
                    it, pl.ds((3 * ky + kx) * 128, 128), :
                ]
        u = dot(a1s[...], e2f[...])
        h2 = (
            u[:, 128:256]
            + jnp.concatenate([zero, u[: ROWS - PITCH, 0:128]], axis=0)
            + jnp.concatenate([u[PITCH:, 256:384], zero], axis=0)
        )
        sig = sigmoid(h2)
        slope2[...] = sig * (1.0 + h2 * (1.0 - sig))
        a2[...] = (h2 * sig).astype(BF16)
        for k in of(2):
            remote(E, it, k).wait_recv()
        relay(W, it, range(N_CHUNKS))
        for j in range(7):
            rs = pl.ds(j * 128, 128)
            pre = dot(a2[rs, :], e3[it]) + x[rs, :].astype(F32)
            sig = sigmoid(pre)
            d3[rs, :] = (cot[rs, :].astype(F32) * (sig * (1.0 + pre * (1.0 - sig)))).astype(BF16)
        if it == 1:
            g3[...] = dot(a2[...].T, d3[...])
            send_grad(it, 2)
        d2 = dot_nt(d3[...], e3[it]) * slope2[...]
        inner = pl.ds(PITCH, ROWS)
        d2s[inner, 0:128] = pltpu.roll(d2, ROWS - 1, 0).astype(BF16)
        d2s[inner, 128:256] = d2.astype(BF16)
        d2s[inner, 256:384] = pltpu.roll(d2, 1, 0).astype(BF16)

        def first():
            t = dot_nt(d2s[inner, :], e2r[...])
            da1 = (
                t[:, 128:256]
                + jnp.concatenate([t[PITCH:, 0:128], zero], axis=0)
                + jnp.concatenate([zero, t[: ROWS - PITCH, 256:384]], axis=0)
            )
            d1 = (da1 * slope1[...]).astype(BF16)
            g1[...] = dot(xt[...], d1)
            send_grad(it, 0)

        def middle():
            for ky in range(3):
                gk = dot(a1t[...], d2s[pl.ds((2 - ky) * PITCH, ROWS), :])
                for kx in range(3):
                    g2[pl.ds((3 * ky + kx) * 128, 128), :] = gk[:, kx * 128 : (kx + 1) * 128]
            send_grad(it, 1)

        if it == 0:
            first()
            middle()
            g3[...] = dot(a2[...].T, d3[...])
            send_grad(it, 2)
            takes, mixes = (0, 1, 2, 3, 4), (0, 1, 2, 3, 4)
        else:
            middle()
            first()
            for k in range(N_CHUNKS):
                remote(W, 1, k).wait_recv()
            takes, mixes = (4, 1, 2, 3, 0), (4, 1, 2, 3, 0)
        lag = 4
        for n in range(N_CHUNKS + lag):
            if n < N_CHUNKS:
                take(it, takes[n])
            if n >= lag:
                relay(M, it, (mixes[n - lag],))
                mix(it, mixes[n - lag])

    for it in range(2):
        for kind in range(4):
            for k in range(N_CHUNKS):
                remote(kind, it, k).wait_send()
        for kind in (W, M):
            relay(kind, it, range(N_CHUNKS), done=True)


def write_out(*refs):
    copies = [pltpu.make_async_copy(refs[i], refs[6 + i], refs[12].at[i]) for i in range(6)]
    for c in copies:
        c.start()
    for c in copies:
        c.wait()


def body(images, cotangent, *state):
    vmem = pl.BlockSpec(memory_space=pltpu.VMEM)
    hbm = pl.BlockSpec(memory_space=pl.ANY)
    pix = (SIDE, SIDE, CIN)
    pair = [pltpu.VMEM((2,) + s, BF16) for s in SHARDS]
    outs = pl.pallas_call(
        kernel,
        out_shape=[jax.ShapeDtypeStruct(s, F32) for s in SHARDS * 2],
        in_specs=[hbm] * 8,
        out_specs=[vmem] * 6,
        scratch_shapes=[
            pltpu.VMEM(pix, BF16), pltpu.VMEM(pix, BF16),
            pltpu.VMEM((ROWS, CIN), BF16), pltpu.VMEM((CIN, ROWS), BF16), pltpu.VMEM((ROWS, CIN), BF16),
            pltpu.VMEM((384, 384), BF16), pltpu.VMEM((384, 384), BF16),
            pltpu.VMEM((ROWS, 384), BF16), pltpu.VMEM((ROWS + 2 * PITCH, 384), BF16),
            pltpu.VMEM((MID, ROWS), BF16), pltpu.VMEM((ROWS, MID), BF16),
            pltpu.VMEM((ROWS, MID), F32), pltpu.VMEM((ROWS, MID), F32),
            pltpu.VMEM((ROWS, CIN), BF16),
        ]
        + [pltpu.VMEM(s, F32) for s in SHARDS] * 2
        + [pltpu.VMEM(s, F32) for s in FULLS]
        + [pltpu.VMEM((2,) + s, BF16) for s in FULLS]
        + pair * 8
        + [
            pltpu.SemaphoreType.DMA((4, 2, N_CHUNKS)),
            pltpu.SemaphoreType.DMA((4, 2, N_CHUNKS)),
            pltpu.SemaphoreType.DMA((8,)),
            pltpu.SemaphoreType.DMA((2, 2, N_CHUNKS)),
            pltpu.SemaphoreType.DMA((2, 2, N_CHUNKS)),
        ],
        compiler_params=pltpu.CompilerParams(
            collective_id=0, has_side_effects=True, vmem_limit_bytes=56 << 20
        ),
    )(images[0], cotangent[0], *[s[0] for s in state])
    outs = pl.pallas_call(
        write_out,
        out_shape=[jax.ShapeDtypeStruct(s, F32) for s in SHARDS * 2],
        in_specs=[pl.BlockSpec(memory_space=pltpu.VMEM)] * 6,
        out_specs=[pl.BlockSpec(memory_space=pltpu.HBM)] * 6,
        scratch_shapes=[pltpu.SemaphoreType.DMA((6,))],
    )(*outs)
    return tuple(o[None] for o in outs)


def solution(mesh):
    pixels = P(("gossip", "dp"), None, None, None)
    rows, columns = P("gossip", "dp", None), P("gossip", None, "dp")
    return jax.shard_map(
        body,
        mesh=mesh,
        in_specs=(pixels, pixels) + (rows, rows, columns) * 2,
        out_specs=(rows, rows, columns) * 2,
        check_vma=False,
    )
```

```python
import functools

import jax
import jax.numpy as jnp
from jax import lax
from jax.experimental import pallas as pl
from jax.experimental.pallas import tpu as pltpu
from jax.sharding import PartitionSpec as P

CIN = 512
MID = 128
SIDE = 28
PITCH = 32
ROWS = SIDE * PITCH
BF16 = jnp.bfloat16
F32 = jnp.float32
MESH = pl.DeviceIdType.MESH
SCALES = (CIN ** (-0.5), (9 * MID) ** (-0.5), MID ** (-0.5))
SHARDS = ((256, 128), (576, 128), (128, 256))
FULLS = ((512, 128), (1152, 128), (128, 512))
learn_rate = 0.1
momentum_coef = 0.9

CHUNKS = ((0, 0, 256), (1, 0, 192), (1, 192, 192), (1, 384, 192), (2, 0, 128))
N_CHUNKS = len(CHUNKS)
E, W, G, M = range(4)
ROUTES = {
    (W, 0): {0: 1, 1: 1, 2: 2, 3: 2, 4: 0},
    (W, 1): {0: 1, 1: 1, 2: 2, 3: 2, 4: 0},
    (M, 0): {3: 2, 4: 1},
    (M, 1): {4: 1, 1: 2, 2: 0},
}


def sigmoid(v):
    return 0.5 * jnp.tanh(0.5 * v) + 0.5


def dot(a, b):
    return jnp.dot(a, b, preferred_element_type=F32)


def dot_nt(a, b):
    return lax.dot_general(a, b, (((1,), (1,)), ((), ())), preferred_element_type=F32)


def half(idx, ref, which, row, rows):
    if idx == 2:
        return ref.at[pl.ds(row, rows), pl.ds(pl.multiple_of(which * 256, 256), 256)]
    start = pl.multiple_of(which * SHARDS[idx][0] + row, 16)
    return ref.at[pl.ds(start, rows), :]


def pad_pixels(src, dst):
    dst[...] = jnp.zeros_like(dst)
    for i in range(SIDE):
        dst[pl.ds(i * PITCH, SIDE), :] = src[i]


def kernel(*refs):
    images, cotangent = refs[0:2]
    w_in, m_in = refs[2:5], refs[5:8]
    w_out, m_out = refs[8:11], refs[11:14]
    (
        x_raw, c_raw, x, xt, cot, e2f, e2r, a1s, d2s, a1t, a2, slope1, slope2, d3,
        w1, w2, w3, m1, m2, m3, g1, g2, g3,
        e1, e2, e3, wb1, wb2, wb3, wa1, wa2, wa3, gb1, gb2, gb3, ga1, ga2, ga3,
        mb1, mb2, mb3, ma1, ma2, ma3,
        rw1, rw2, rw3, rm1, rm2, rm3, send_sem, recv_sem, in_sem, relay_send, relay_recv, out_sem,
    ) = refs[14:]
    w, m, g, e = (w1, w2, w3), (m1, m2, m3), (g1, g2, g3), (e1, e2, e3)
    wb, wa, gb, ga, mb, ma = (
        (wb1, wb2, wb3), (wa1, wa2, wa3), (gb1, gb2, gb3), (ga1, ga2, ga3),
        (mb1, mb2, mb3), (ma1, ma2, ma3),
    )
    me, dp = lax.axis_index("gossip"), lax.axis_index("dp")
    count = lax.axis_size("gossip")

    def at(steps):
        return (lax.rem(me + steps + count, count), dp)

    partner = (me, 1 - dp)
    core, spot = lax.rem(me, 2), lax.rem(me, 64) // 2
    x_lo = me // 64
    far = 64 * (1 - x_lo)
    last, origin = spot == 31, spot == 0
    relays = (spot == 7) | (spot == 15) | (spot == 23)
    relay_bufs = {W: (rw1, rw2, rw3), M: (rm1, rm2, rm3)}

    barrier = pltpu.get_barrier_semaphore()
    for other in (partner, at(1), at(-1), at(2), at(-2)):
        pl.semaphore_signal(barrier, inc=1, device_id=other, device_id_type=MESH)

    def greet(other):
        pl.semaphore_signal(barrier, inc=1, device_id=(other, dp), device_id_type=MESH)

    @pl.when(last)
    def _():
        for y in range(3):
            greet(64 * x_lo + 16 * y + 14 + core)

    @pl.when(relays)
    def _():
        greet(64 * x_lo + 62 + core)
        greet(far + core)

        @pl.when(core == 1)
        def _():
            greet(far)

    @pl.when(origin)
    def _():
        for y in range(3):
            greet(far + 16 * y + 14 + core)

            @pl.when(core == 0)
            def _():
                greet(far + 16 * y + 15)

    guests = 5 + jnp.where(last, 3, 0) + jnp.where(relays, 2 + core, 0) + jnp.where(origin, 6 - 3 * core, 0)
    loads = {}
    for n, (src, dst) in enumerate(
        list(zip(w_in, w)) + [(images, x_raw), (cotangent, c_raw)] + list(zip(m_in, m))
    ):
        loads[n] = pltpu.make_async_copy(src, dst, in_sem.at[n])
        loads[n].start()

    def remote(kind, it, k):
        idx, row, rows = CHUNKS[k]
        rs = pl.ds(row, rows)
        if kind == E:
            src = half(idx, e[idx].at[it], dp, row, rows)
            dst, to = src, partner
        elif kind == W:
            src, dst, to = wb[idx].at[it, rs, :], wa[idx].at[it, rs, :], at(it + 1)
        elif kind == G:
            src, dst, to = gb[idx].at[it, rs, :], ga[idx].at[it, rs, :], partner
        else:
            src, dst, to = mb[idx].at[it, rs, :], ma[idx].at[it, rs, :], at(it + 1)
        return pltpu.make_async_remote_copy(
            src_ref=src, dst_ref=dst, send_sem=send_sem.at[kind, it, k],
            recv_sem=recv_sem.at[kind, it, k], device_id=to, device_id_type=MESH,
        )

    def to_relay(kind, it, k):
        idx, row, rows = CHUNKS[k]
        rs = pl.ds(row, rows)
        src = {W: wb, M: mb}[kind][idx].at[it, rs, :]
        y = ROUTES[kind, it][k]
        return pltpu.make_async_remote_copy(
            src_ref=src, dst_ref=relay_bufs[kind][idx].at[it, rs, :],
            send_sem=send_sem.at[kind, it, k], recv_sem=relay_recv.at[kind // 2, it, k],
            device_id=(64 * x_lo + 16 * y + 14 + core, dp), device_id_type=MESH,
        )

    def from_relay(kind, it, k):
        idx, row, rows = CHUNKS[k]
        rs = pl.ds(row, rows)
        return pltpu.make_async_remote_copy(
            src_ref=relay_bufs[kind][idx].at[it, rs, :], dst_ref={W: wa, M: ma}[kind][idx].at[it, rs, :],
            send_sem=relay_send.at[kind // 2, it, k], recv_sem=recv_sem.at[kind, it, k],
            device_id=(far + it * core, dp), device_id_type=MESH,
        )

    def active(it, where):
        return where if it == 1 else where & (core == 1)

    def gossip(kind, it, k):
        if k not in ROUTES[kind, it]:
            remote(kind, it, k).start()
            return
        cross = active(it, last)

        @pl.when(cross)
        def _():
            to_relay(kind, it, k).start()

        @pl.when(jnp.logical_not(cross))
        def _():
            remote(kind, it, k).start()

    def relay(kind, it, chunks, done=False):
        for y in range(3):
            mine = [k for k in chunks if ROUTES[kind, it].get(k) == y]
            if mine:

                @pl.when(active(it, spot == 8 * y + 7))
                def _():
                    for k in mine:
                        if done:
                            from_relay(kind, it, k).wait_send()
                        else:
                            to_relay(kind, it, k).wait_recv()
                            from_relay(kind, it, k).start()

    def store(k):
        idx, row, rows = CHUNKS[k]
        rs = pl.ds(row, rows)
        return (
            pltpu.make_async_copy(w[idx].at[rs, :], w_out[idx].at[rs, :], out_sem.at[0, k]),
            pltpu.make_async_copy(m[idx].at[rs, :], m_out[idx].at[rs, :], out_sem.at[1, k]),
        )

    def of(idx):
        return [k for k in range(N_CHUNKS) if CHUNKS[k][0] == idx]

    for idx in range(3):
        loads[idx].wait()
        full = (0, SHARDS[idx][0])
        half(idx, e[idx].at[0], dp, *full)[...] = (w[idx][...] * SCALES[idx]).astype(BF16)
        wb[idx][0] = w[idx][...].astype(BF16)
    pl.semaphore_wait(barrier, guests)
    for k in range(N_CHUNKS):
        remote(E, 0, k).start()
    for k in range(N_CHUNKS):
        gossip(W, 0, k)

    d2s[...] = jnp.zeros_like(d2s)
    loads[3].wait()
    pad_pixels(x_raw, x)
    xt[...] = x[...].T
    loads[4].wait()
    pad_pixels(c_raw, cot)
    for n in range(5, 8):
        loads[n].wait()

    zero = jnp.zeros((PITCH, MID), F32)

    def take(it, k):
        idx, row, rows = CHUNKS[k]
        rs = pl.ds(row, rows)
        remote(G, it, k).wait_recv()
        total = half(idx, g[idx], dp, row, rows)[...] + ga[idx][it, rs, :].astype(F32)
        new = momentum_coef * m[idx][rs, :] + SCALES[idx] * total
        m[idx][rs, :] = new
        mb[idx][it, rs, :] = new.astype(BF16)
        gossip(M, it, k)

    def mix(it, k):
        idx, row, rows = CHUNKS[k]
        rs = pl.ds(row, rows)
        remote(M, it, k).wait_recv()
        mean = 0.5 * (m[idx][rs, :] + ma[idx][it, rs, :].astype(F32))
        if it == 0:
            remote(W, it, k).wait_recv()
        weight = 0.5 * (w[idx][rs, :] + wa[idx][it, rs, :].astype(F32)) - learn_rate * mean
        m[idx][rs, :] = mean
        w[idx][rs, :] = weight
        if it == 0:
            half(idx, e[idx].at[1], dp, row, rows)[...] = (weight * SCALES[idx]).astype(BF16)
            remote(E, 1, k).start()
            wb[idx][1, rs, :] = weight.astype(BF16)
            gossip(W, 1, k)
        else:
            for copy in store(k):
                copy.start()

    def send_grad(it, idx):
        for k in of(idx):
            _, row, rows = CHUNKS[k]
            gb[idx][it, pl.ds(row, rows), :] = half(idx, g[idx], 1 - dp, row, rows)[...].astype(BF16)
            remote(G, it, k).start()

    for it in range(2):
        for k in of(0):
            remote(E, it, k).wait_recv()
        h1 = dot(x[...], e1[it])
        sig = sigmoid(h1)
        act1 = h1 * sig
        slope1[...] = sig * (1.0 + h1 * (1.0 - sig))
        a1s[:, 0:128] = pltpu.roll(act1, 1, 0).astype(BF16)
        a1s[:, 128:256] = act1.astype(BF16)
        a1s[:, 256:384] = pltpu.roll(act1, ROWS - 1, 0).astype(BF16)
        a1t[...] = act1.astype(BF16).T
        for k in of(1):
            remote(E, it, k).wait_recv()
        for ky in range(3):
            e2f[:, ky * 128 : (ky + 1) * 128] = e2[it, pl.ds(ky * 384, 384), :]
            for kx in range(3):
                e2r[pl.ds(ky * 128, 128), kx * 128 : (kx + 1) * 128] = e2[
                    it, pl.ds((3 * ky + kx) * 128, 128), :
                ]
        u = dot(a1s[...], e2f[...])
        h2 = (
            u[:, 128:256]
            + jnp.concatenate([zero, u[: ROWS - PITCH, 0:128]], axis=0)
            + jnp.concatenate([u[PITCH:, 256:384], zero], axis=0)
        )
        sig = sigmoid(h2)
        slope2[...] = sig * (1.0 + h2 * (1.0 - sig))
        a2[...] = (h2 * sig).astype(BF16)
        def out_half(which):
            cols = pl.ds(pl.multiple_of(which * 256, 256), 256)
            for j in range(7):
                rs = pl.ds(j * 128, 128)
                pre = dot(a2[rs, :], e3[it, :, cols]) + x[rs, cols].astype(F32)
                sig = sigmoid(pre)
                d3[rs, cols] = (cot[rs, cols].astype(F32) * (sig * (1.0 + pre * (1.0 - sig)))).astype(BF16)
            return dot_nt(d3[:, cols], e3[it, :, cols])

        da2 = out_half(dp)
        for k in of(2):
            remote(E, it, k).wait_recv()
        relay(W, it, range(N_CHUNKS))
        da2 = da2 + out_half(1 - dp)
        if it == 1:
            g3[...] = dot(a2[...].T, d3[...])
            send_grad(it, 2)
        d2 = da2 * slope2[...]
        inner = pl.ds(PITCH, ROWS)
        d2s[inner, 0:128] = pltpu.roll(d2, ROWS - 1, 0).astype(BF16)
        d2s[inner, 128:256] = d2.astype(BF16)
        d2s[inner, 256:384] = pltpu.roll(d2, 1, 0).astype(BF16)

        def first():
            t = dot_nt(d2s[inner, :], e2r[...])
            da1 = (
                t[:, 128:256]
                + jnp.concatenate([t[PITCH:, 0:128], zero], axis=0)
                + jnp.concatenate([zero, t[: ROWS - PITCH, 256:384]], axis=0)
            )
            d1 = (da1 * slope1[...]).astype(BF16)
            g1[...] = dot(xt[...], d1)
            send_grad(it, 0)

        def middle():
            for ky in range(3):
                gk = dot(a1t[...], d2s[pl.ds((2 - ky) * PITCH, ROWS), :])
                for kx in range(3):
                    g2[pl.ds((3 * ky + kx) * 128, 128), :] = gk[:, kx * 128 : (kx + 1) * 128]
            send_grad(it, 1)

        if it == 0:
            first()
            middle()
            g3[...] = dot(a2[...].T, d3[...])
            send_grad(it, 2)
            takes, mixes = (0, 1, 2, 3, 4), (0, 1, 2, 3, 4)
        else:
            middle()
            first()
            for k in range(N_CHUNKS):
                remote(W, 1, k).wait_recv()
            takes, mixes = (4, 1, 2, 3, 0), (4, 1, 2, 3, 0)
        lag = 4
        for n in range(N_CHUNKS + lag):
            if n < N_CHUNKS:
                take(it, takes[n])
            if n >= lag:
                relay(M, it, (mixes[n - lag],))
                mix(it, mixes[n - lag])

    for k in range(N_CHUNKS):
        for copy in store(k):
            copy.wait()
    for it in range(2):
        for kind in range(4):
            for k in range(N_CHUNKS):
                remote(kind, it, k).wait_send()
        for kind in (W, M):
            relay(kind, it, range(N_CHUNKS), done=True)


def write_out(*refs):
    sem = refs[18]
    loads = [pltpu.make_async_copy(refs[i], refs[12 + i], sem.at[0, i]) for i in range(6)]
    stores = [pltpu.make_async_copy(refs[12 + i], refs[6 + i], sem.at[1, i]) for i in range(6)]
    for copy in loads:
        copy.start()
    for load, copy in zip(loads, stores):
        load.wait()
        copy.start()
    for copy in stores:
        copy.wait()


def body(images, cotangent, *state):
    hbm = pl.BlockSpec(memory_space=pl.ANY)
    pix = (SIDE, SIDE, CIN)
    pair = [pltpu.VMEM((2,) + s, BF16) for s in SHARDS]
    outs = pl.pallas_call(
        kernel,
        out_shape=[jax.ShapeDtypeStruct(s, F32) for s in SHARDS * 2],
        in_specs=[hbm] * 8,
        out_specs=[hbm] * 6,
        scratch_shapes=[
            pltpu.VMEM(pix, BF16), pltpu.VMEM(pix, BF16),
            pltpu.VMEM((ROWS, CIN), BF16), pltpu.VMEM((CIN, ROWS), BF16), pltpu.VMEM((ROWS, CIN), BF16),
            pltpu.VMEM((384, 384), BF16), pltpu.VMEM((384, 384), BF16),
            pltpu.VMEM((ROWS, 384), BF16), pltpu.VMEM((ROWS + 2 * PITCH, 384), BF16),
            pltpu.VMEM((MID, ROWS), BF16), pltpu.VMEM((ROWS, MID), BF16),
            pltpu.VMEM((ROWS, MID), F32), pltpu.VMEM((ROWS, MID), F32),
            pltpu.VMEM((ROWS, CIN), BF16),
        ]
        + [pltpu.VMEM(s, F32) for s in SHARDS] * 2
        + [pltpu.VMEM(s, F32) for s in FULLS]
        + [pltpu.VMEM((2,) + s, BF16) for s in FULLS]
        + pair * 8
        + [
            pltpu.SemaphoreType.DMA((4, 2, N_CHUNKS)),
            pltpu.SemaphoreType.DMA((4, 2, N_CHUNKS)),
            pltpu.SemaphoreType.DMA((8,)),
            pltpu.SemaphoreType.DMA((2, 2, N_CHUNKS)),
            pltpu.SemaphoreType.DMA((2, 2, N_CHUNKS)),
            pltpu.SemaphoreType.DMA((2, N_CHUNKS)),
        ],
        compiler_params=pltpu.CompilerParams(
            collective_id=0, has_side_effects=True, vmem_limit_bytes=56 << 20
        ),
    )(images[0], cotangent[0], *[s[0] for s in state])
    outs = pl.pallas_call(
        write_out,
        out_shape=[jax.ShapeDtypeStruct(s, F32) for s in SHARDS * 2],
        in_specs=[hbm] * 6,
        out_specs=[hbm] * 6,
        scratch_shapes=[pltpu.VMEM(s, F32) for s in SHARDS * 2] + [pltpu.SemaphoreType.DMA((2, 6))],
        compiler_params=pltpu.CompilerParams(vmem_limit_bytes=60 << 20),
    )(*outs)
    return tuple(o[None] for o in outs)


def solution(mesh):
    pixels = P(("gossip", "dp"), None, None, None)
    rows, columns = P("gossip", "dp", None), P("gossip", None, "dp")
    return jax.shard_map(
        body,
        mesh=mesh,
        in_specs=(pixels, pixels) + (rows, rows, columns) * 2,
        out_specs=(rows, rows, columns) * 2,
        check_vma=False,
    )
```

```python
import functools

import jax
import jax.numpy as jnp
from jax import lax
from jax.experimental import pallas as pl
from jax.experimental.pallas import tpu as pltpu
from jax.sharding import PartitionSpec as P

CIN = 512
MID = 128
SIDE = 28
PITCH = 32
ROWS = SIDE * PITCH
BF16 = jnp.bfloat16
F32 = jnp.float32
MESH = pl.DeviceIdType.MESH
SCALES = (CIN ** (-0.5), (9 * MID) ** (-0.5), MID ** (-0.5))
SHARDS = ((256, 128), (576, 128), (128, 256))
FULLS = ((512, 128), (1152, 128), (128, 512))
learn_rate = 0.1
momentum_coef = 0.9

CHUNKS = ((0, 0, 256), (1, 0, 192), (1, 192, 192), (1, 384, 192), (2, 0, 128))
N_CHUNKS = len(CHUNKS)
E, W, G, M = range(4)
ROUTES = {
    (W, 0): {0: 1, 1: 1, 2: 2, 3: 2, 4: 0},
    (W, 1): {0: 1, 1: 1, 2: 2, 3: 2, 4: 0},
    (M, 0): {3: 2, 4: 1},
    (M, 1): {4: 1, 1: 2, 2: 0},
}


def sigmoid(v):
    return 0.5 * jnp.tanh(0.5 * v) + 0.5


def dot(a, b):
    return jnp.dot(a, b, preferred_element_type=F32)


def dot_nt(a, b):
    return lax.dot_general(a, b, (((1,), (1,)), ((), ())), preferred_element_type=F32)


def half(idx, ref, which, row, rows):
    if idx == 2:
        return ref.at[pl.ds(row, rows), pl.ds(pl.multiple_of(which * 256, 256), 256)]
    start = pl.multiple_of(which * SHARDS[idx][0] + row, 16)
    return ref.at[pl.ds(start, rows), :]


def pad_pixels(src, dst):
    dst[...] = jnp.zeros_like(dst)
    for i in range(SIDE):
        dst[pl.ds(i * PITCH, SIDE), :] = src[i]


def kernel(*refs):
    images, cotangent = refs[0:2]
    w_in, m_in = refs[2:5], refs[5:8]
    w_out, m_out = refs[8:11], refs[11:14]
    (
        x_raw, c_raw, x, xt, cot, e2f, e2r, a1s, d2s, a1t, a2, slope1, slope2, d3,
        w1, w2, w3, m1, m2, m3, g1, g2, g3,
        e1, e2, e3, wb1, wb2, wb3, wa1, wa2, wa3, gb1, gb2, gb3, ga1, ga2, ga3,
        mb1, mb2, mb3, ma1, ma2, ma3,
        rw1, rw2, rw3, rm1, rm2, rm3, send_sem, recv_sem, in_sem, relay_send, relay_recv, out_sem,
    ) = refs[14:]
    w, m, g, e = (w1, w2, w3), (m1, m2, m3), (g1, g2, g3), (e1, e2, e3)
    wb, wa, gb, ga, mb, ma = (
        (wb1, wb2, wb3), (wa1, wa2, wa3), (gb1, gb2, gb3), (ga1, ga2, ga3),
        (mb1, mb2, mb3), (ma1, ma2, ma3),
    )
    me, dp = lax.axis_index("gossip"), lax.axis_index("dp")
    count = lax.axis_size("gossip")

    def at(steps):
        return (lax.rem(me + steps + count, count), dp)

    partner = (me, 1 - dp)
    core, spot = lax.rem(me, 2), lax.rem(me, 64) // 2
    x_lo = me // 64
    far = 64 * (1 - x_lo)
    last, origin = spot == 31, spot == 0
    relays = (spot == 7) | (spot == 15) | (spot == 23)
    relay_bufs = {W: (rw1, rw2, rw3), M: (rm1, rm2, rm3)}

    barrier = pltpu.get_barrier_semaphore()
    for other in (partner, at(1), at(-1), at(2), at(-2)):
        pl.semaphore_signal(barrier, inc=1, device_id=other, device_id_type=MESH)

    def greet(other):
        pl.semaphore_signal(barrier, inc=1, device_id=(other, dp), device_id_type=MESH)

    @pl.when(last)
    def _():
        for y in range(3):
            greet(64 * x_lo + 16 * y + 14 + core)

    @pl.when(relays)
    def _():
        greet(64 * x_lo + 62 + core)
        greet(far + core)

        @pl.when(core == 1)
        def _():
            greet(far)

    @pl.when(origin)
    def _():
        for y in range(3):
            greet(far + 16 * y + 14 + core)

            @pl.when(core == 0)
            def _():
                greet(far + 16 * y + 15)

    guests = 5 + jnp.where(last, 3, 0) + jnp.where(relays, 2 + core, 0) + jnp.where(origin, 6 - 3 * core, 0)
    loads = {}
    for n, (src, dst) in enumerate(
        list(zip(w_in, w)) + [(images, x_raw), (cotangent, c_raw)] + list(zip(m_in, m))
    ):
        loads[n] = pltpu.make_async_copy(src, dst, in_sem.at[n])
        loads[n].start()

    def remote(kind, it, k):
        idx, row, rows = CHUNKS[k]
        rs = pl.ds(row, rows)
        if kind == E:
            src = half(idx, e[idx].at[it], dp, row, rows)
            dst, to = src, partner
        elif kind == W:
            src, dst, to = wb[idx].at[it, rs, :], wa[idx].at[it, rs, :], at(it + 1)
        elif kind == G:
            src, dst, to = gb[idx].at[it, rs, :], ga[idx].at[it, rs, :], partner
        else:
            src, dst, to = mb[idx].at[it, rs, :], ma[idx].at[it, rs, :], at(it + 1)
        return pltpu.make_async_remote_copy(
            src_ref=src, dst_ref=dst, send_sem=send_sem.at[kind, it, k],
            recv_sem=recv_sem.at[kind, it, k], device_id=to, device_id_type=MESH,
        )

    def to_relay(kind, it, k):
        idx, row, rows = CHUNKS[k]
        rs = pl.ds(row, rows)
        src = {W: wb, M: mb}[kind][idx].at[it, rs, :]
        y = ROUTES[kind, it][k]
        return pltpu.make_async_remote_copy(
            src_ref=src, dst_ref=relay_bufs[kind][idx].at[it, rs, :],
            send_sem=send_sem.at[kind, it, k], recv_sem=relay_recv.at[kind // 2, it, k],
            device_id=(64 * x_lo + 16 * y + 14 + core, dp), device_id_type=MESH,
        )

    def from_relay(kind, it, k):
        idx, row, rows = CHUNKS[k]
        rs = pl.ds(row, rows)
        return pltpu.make_async_remote_copy(
            src_ref=relay_bufs[kind][idx].at[it, rs, :], dst_ref={W: wa, M: ma}[kind][idx].at[it, rs, :],
            send_sem=relay_send.at[kind // 2, it, k], recv_sem=recv_sem.at[kind, it, k],
            device_id=(far + it * core, dp), device_id_type=MESH,
        )

    def active(it, where):
        return where if it == 1 else where & (core == 1)

    def gossip(kind, it, k):
        if k not in ROUTES[kind, it]:
            remote(kind, it, k).start()
            return
        cross = active(it, last)

        @pl.when(cross)
        def _():
            to_relay(kind, it, k).start()

        @pl.when(jnp.logical_not(cross))
        def _():
            remote(kind, it, k).start()

    def relay(kind, it, chunks, done=False):
        for y in range(3):
            mine = [k for k in chunks if ROUTES[kind, it].get(k) == y]
            if mine:

                @pl.when(active(it, spot == 8 * y + 7))
                def _():
                    for k in mine:
                        if done:
                            from_relay(kind, it, k).wait_send()
                        else:
                            to_relay(kind, it, k).wait_recv()
                            from_relay(kind, it, k).start()

    def store(k):
        idx, row, rows = CHUNKS[k]
        rs = pl.ds(row, rows)
        return (
            pltpu.make_async_copy(w[idx].at[rs, :], w_out[idx].at[rs, :], out_sem.at[0, k]),
            pltpu.make_async_copy(m[idx].at[rs, :], m_out[idx].at[rs, :], out_sem.at[1, k]),
        )

    def of(idx):
        return [k for k in range(N_CHUNKS) if CHUNKS[k][0] == idx]

    for idx in range(3):
        loads[idx].wait()
        full = (0, SHARDS[idx][0])
        half(idx, e[idx].at[0], dp, *full)[...] = (w[idx][...] * SCALES[idx]).astype(BF16)
        wb[idx][0] = w[idx][...].astype(BF16)
    pl.semaphore_wait(barrier, guests)
    for k in range(N_CHUNKS):
        remote(E, 0, k).start()
    for k in range(N_CHUNKS):
        gossip(W, 0, k)

    d2s[...] = jnp.zeros_like(d2s)
    loads[3].wait()
    pad_pixels(x_raw, x)
    xt[...] = x[...].T
    loads[4].wait()
    pad_pixels(c_raw, cot)
    for n in range(5, 8):
        loads[n].wait()

    zero = jnp.zeros((PITCH, MID), F32)

    def take(it, k):
        idx, row, rows = CHUNKS[k]
        rs = pl.ds(row, rows)
        remote(G, it, k).wait_recv()
        total = half(idx, g[idx], dp, row, rows)[...] + ga[idx][it, rs, :].astype(F32)
        new = momentum_coef * m[idx][rs, :] + SCALES[idx] * total
        m[idx][rs, :] = new
        mb[idx][it, rs, :] = new.astype(BF16)
        gossip(M, it, k)

    def mix(it, k):
        idx, row, rows = CHUNKS[k]
        rs = pl.ds(row, rows)
        remote(M, it, k).wait_recv()
        mean = 0.5 * (m[idx][rs, :] + ma[idx][it, rs, :].astype(F32))
        if it == 0:
            remote(W, it, k).wait_recv()
        weight = 0.5 * (w[idx][rs, :] + wa[idx][it, rs, :].astype(F32)) - learn_rate * mean
        m[idx][rs, :] = mean
        w[idx][rs, :] = weight
        if it == 0:
            half(idx, e[idx].at[1], dp, row, rows)[...] = (weight * SCALES[idx]).astype(BF16)
            remote(E, 1, k).start()
            wb[idx][1, rs, :] = weight.astype(BF16)
            gossip(W, 1, k)
        else:
            for copy in store(k):
                copy.start()

    def send_grad(it, idx):
        for k in of(idx):
            _, row, rows = CHUNKS[k]
            gb[idx][it, pl.ds(row, rows), :] = half(idx, g[idx], 1 - dp, row, rows)[...].astype(BF16)
            remote(G, it, k).start()

    for it in range(2):
        def in_half(which):
            chans = pl.ds(pl.multiple_of(which * 256, 256), 256)
            return dot(x[:, chans], e1[it, chans, :])

        h1 = in_half(dp)
        for k in of(0):
            remote(E, it, k).wait_recv()
        h1 = h1 + in_half(1 - dp)
        sig = sigmoid(h1)
        act1 = h1 * sig
        slope1[...] = sig * (1.0 + h1 * (1.0 - sig))
        a1s[:, 0:128] = pltpu.roll(act1, 1, 0).astype(BF16)
        a1s[:, 128:256] = act1.astype(BF16)
        a1s[:, 256:384] = pltpu.roll(act1, ROWS - 1, 0).astype(BF16)
        a1t[...] = act1.astype(BF16).T
        for k in of(1):
            remote(E, it, k).wait_recv()
        for ky in range(3):
            e2f[:, ky * 128 : (ky + 1) * 128] = e2[it, pl.ds(ky * 384, 384), :]
            for kx in range(3):
                e2r[pl.ds(ky * 128, 128), kx * 128 : (kx + 1) * 128] = e2[
                    it, pl.ds((3 * ky + kx) * 128, 128), :
                ]
        u = dot(a1s[...], e2f[...])
        h2 = (
            u[:, 128:256]
            + jnp.concatenate([zero, u[: ROWS - PITCH, 0:128]], axis=0)
            + jnp.concatenate([u[PITCH:, 256:384], zero], axis=0)
        )
        sig = sigmoid(h2)
        slope2[...] = sig * (1.0 + h2 * (1.0 - sig))
        a2[...] = (h2 * sig).astype(BF16)
        def out_half(which):
            cols = pl.ds(pl.multiple_of(which * 256, 256), 256)
            for j in range(7):
                rs = pl.ds(j * 128, 128)
                pre = dot(a2[rs, :], e3[it, :, cols]) + x[rs, cols].astype(F32)
                sig = sigmoid(pre)
                d3[rs, cols] = (cot[rs, cols].astype(F32) * (sig * (1.0 + pre * (1.0 - sig)))).astype(BF16)
            return dot_nt(d3[:, cols], e3[it, :, cols])

        da2 = out_half(dp)
        for k in of(2):
            remote(E, it, k).wait_recv()
        relay(W, it, range(N_CHUNKS))
        da2 = da2 + out_half(1 - dp)
        if it == 1:
            g3[...] = dot(a2[...].T, d3[...])
            send_grad(it, 2)
        d2 = da2 * slope2[...]
        inner = pl.ds(PITCH, ROWS)
        d2s[inner, 0:128] = pltpu.roll(d2, ROWS - 1, 0).astype(BF16)
        d2s[inner, 128:256] = d2.astype(BF16)
        d2s[inner, 256:384] = pltpu.roll(d2, 1, 0).astype(BF16)

        def first():
            t = dot_nt(d2s[inner, :], e2r[...])
            da1 = (
                t[:, 128:256]
                + jnp.concatenate([t[PITCH:, 0:128], zero], axis=0)
                + jnp.concatenate([zero, t[: ROWS - PITCH, 256:384]], axis=0)
            )
            d1 = (da1 * slope1[...]).astype(BF16)
            g1[...] = dot(xt[...], d1)
            send_grad(it, 0)

        def middle():
            for ky in range(3):
                gk = dot(a1t[...], d2s[pl.ds((2 - ky) * PITCH, ROWS), :])
                for kx in range(3):
                    g2[pl.ds((3 * ky + kx) * 128, 128), :] = gk[:, kx * 128 : (kx + 1) * 128]
            send_grad(it, 1)

        if it == 0:
            first()
            middle()
            g3[...] = dot(a2[...].T, d3[...])
            send_grad(it, 2)
            takes, mixes = (0, 1, 2, 3, 4), (0, 1, 2, 3, 4)
        else:
            middle()
            first()
            for k in range(N_CHUNKS):
                remote(W, 1, k).wait_recv()
            takes, mixes = (4, 1, 2, 3, 0), (4, 1, 2, 3, 0)
        lag = 4
        for n in range(N_CHUNKS + lag):
            if n < N_CHUNKS:
                take(it, takes[n])
            if n >= lag:
                relay(M, it, (mixes[n - lag],))
                mix(it, mixes[n - lag])

    for k in range(N_CHUNKS):
        for copy in store(k):
            copy.wait()
    for it in range(2):
        for kind in range(4):
            for k in range(N_CHUNKS):
                remote(kind, it, k).wait_send()
        for kind in (W, M):
            relay(kind, it, range(N_CHUNKS), done=True)


def write_out(*refs):
    sem = refs[18]
    loads = [pltpu.make_async_copy(refs[i], refs[12 + i], sem.at[0, i]) for i in range(6)]
    stores = [pltpu.make_async_copy(refs[12 + i], refs[6 + i], sem.at[1, i]) for i in range(6)]
    for copy in loads:
        copy.start()
    for load, copy in zip(loads, stores):
        load.wait()
        copy.start()
    for copy in stores:
        copy.wait()


def body(images, cotangent, *state):
    hbm = pl.BlockSpec(memory_space=pl.ANY)
    pix = (SIDE, SIDE, CIN)
    pair = [pltpu.VMEM((2,) + s, BF16) for s in SHARDS]
    outs = pl.pallas_call(
        kernel,
        out_shape=[jax.ShapeDtypeStruct(s, F32) for s in SHARDS * 2],
        in_specs=[hbm] * 8,
        out_specs=[hbm] * 6,
        scratch_shapes=[
            pltpu.VMEM(pix, BF16), pltpu.VMEM(pix, BF16),
            pltpu.VMEM((ROWS, CIN), BF16), pltpu.VMEM((CIN, ROWS), BF16), pltpu.VMEM((ROWS, CIN), BF16),
            pltpu.VMEM((384, 384), BF16), pltpu.VMEM((384, 384), BF16),
            pltpu.VMEM((ROWS, 384), BF16), pltpu.VMEM((ROWS + 2 * PITCH, 384), BF16),
            pltpu.VMEM((MID, ROWS), BF16), pltpu.VMEM((ROWS, MID), BF16),
            pltpu.VMEM((ROWS, MID), F32), pltpu.VMEM((ROWS, MID), F32),
            pltpu.VMEM((ROWS, CIN), BF16),
        ]
        + [pltpu.VMEM(s, F32) for s in SHARDS] * 2
        + [pltpu.VMEM(s, F32) for s in FULLS]
        + [pltpu.VMEM((2,) + s, BF16) for s in FULLS]
        + pair * 8
        + [
            pltpu.SemaphoreType.DMA((4, 2, N_CHUNKS)),
            pltpu.SemaphoreType.DMA((4, 2, N_CHUNKS)),
            pltpu.SemaphoreType.DMA((8,)),
            pltpu.SemaphoreType.DMA((2, 2, N_CHUNKS)),
            pltpu.SemaphoreType.DMA((2, 2, N_CHUNKS)),
            pltpu.SemaphoreType.DMA((2, N_CHUNKS)),
        ],
        compiler_params=pltpu.CompilerParams(
            collective_id=0, has_side_effects=True, vmem_limit_bytes=56 << 20
        ),
    )(images[0], cotangent[0], *[s[0] for s in state])
    outs = pl.pallas_call(
        write_out,
        out_shape=[jax.ShapeDtypeStruct(s, F32) for s in SHARDS * 2],
        in_specs=[hbm] * 6,
        out_specs=[hbm] * 6,
        scratch_shapes=[pltpu.VMEM(s, F32) for s in SHARDS * 2] + [pltpu.SemaphoreType.DMA((2, 6))],
        compiler_params=pltpu.CompilerParams(vmem_limit_bytes=60 << 20),
    )(*outs)
    return tuple(o[None] for o in outs)


def solution(mesh):
    pixels = P(("gossip", "dp"), None, None, None)
    rows, columns = P("gossip", "dp", None), P("gossip", None, "dp")
    return jax.shard_map(
        body,
        mesh=mesh,
        in_specs=(pixels, pixels) + (rows, rows, columns) * 2,
        out_specs=(rows, rows, columns) * 2,
        check_vma=False,
    )
```
